32 devices in a mesh: high: 4 (over y, core), mid: 8 (over z, x).
Axes of the slice: x: 2, y: 2, z: 4, core: 2. Of those that a mesh axis runs over, the one named last changes fastest.
Arguments:
- amplitudes: float32 [2, 4, 8, 524288], P(None, 'high', 'mid'), may hold values from -6 to 6
- layer_gates: float32 [4, 2, 128, 128], replicated, may hold values from -0.375 to 0.375
- ctrl_gate: float32 [2, 64, 64], replicated, may hold values from -0.5 to 0.5
- control_mask: int32 [4, 8, 8192], P('high', 'mid'), may hold values 0 or 1
- mid_angles: float32 [3], replicated, may hold values from -3.140625 to 3.140625
Outputs:
- final_state: float32 [2, 4, 8, 524288], P(None, 'high', 'mid')
The draws below stay inside these ranges and needn't reach their ends.
All inputs are finite; a program needn't handle non-finite values. No bound on the sum of `control_mask` on one device may be relied on, other than what follows from the above.
Results may differ from the reference program's by a relative error of at most 0.0003.
Values sent between devices are 32-bit elements; how exact they have to be, the bound alone decides.
No kernel may reach another device: no remote copies, remote signals or barrier semaphores. Data moves between devices by JAX's collectives and lax.ppermute only.
A program may use at most 64 MiB of HBM per device.

```python
import jax
import jax.numpy as jnp
from jax import lax

LOCAL = 524288
GATE = 128
BLOCK = 64
LAYERS = 4
N_HIGH = 4
N_MID = 8


def with_ends(array, own_key, low, high):
    shape = array.shape
    index_at = [jax.random.randint(jax.random.fold_in(own_key, axis), (), 0, shape[axis]) for axis in range(len(shape))]
    array = array.at[tuple(index_at)].set(low)
    longest = shape.index(max(shape))
    index_at[longest] = (index_at[longest] + 1) % shape[longest]
    return array.at[tuple(index_at)].set(high)


def levels(own_key, dims, split, low, high):
    def one(axis_at, blocks):
        draws = jax.random.uniform(jax.random.fold_in(jax.random.fold_in(own_key, 6), axis_at), (blocks,), jnp.float32, low / len(split), high / len(split))
        return jnp.repeat(jnp.exp(draws), dims[axis_at] // blocks).reshape((-1,) + (1,) * (len(dims) - axis_at - 1))

    level = one(*split[0])
    for cut in split[1:]:
        level = level * one(*cut)
    return level


def noise(key, shape, deviation, bound, pieces=(), dtype=jnp.bfloat16):
    values = deviation * jax.random.normal(key, shape, jnp.float32)
    if pieces:
        values = values * levels(key, shape, pieces, -0.22, 0.18)
    return jnp.clip(values, -bound, bound).astype(dtype)


def setup_inputs(seed: int = 0) -> dict:
    keys = jax.random.split(jax.random.key(seed), 6)
    return {
        "amplitudes": noise(keys[0], (2, N_HIGH, N_MID, LOCAL), 1.0, 6.0, ((1, 4), (2, 8)), jnp.float32),
        "layer_gates": noise(keys[1], (LAYERS, 2, GATE, GATE), (2 * GATE) ** -0.5, 0.375, (), jnp.float32),
        "ctrl_gate": noise(keys[2], (2, BLOCK, BLOCK), (2 * BLOCK) ** -0.5, 0.5, (), jnp.float32),
        "control_mask": with_ends((jax.random.randint(keys[3], (N_HIGH, N_MID, LOCAL // BLOCK), 0, 2) < 1).astype(jnp.int32), jax.random.fold_in(keys[3], 1), 0, 1),
        "mid_angles": jnp.clip(jax.random.uniform(keys[4], (3,), jnp.float32, -3.140625, 3.140625), -3.140625, 3.140625),
    }


top_precision = lax.Precision.HIGHEST


def twisted(formula, gate_real, gate_imag, real_part, imag_part):
    out_real = jnp.einsum(formula, gate_real, real_part, precision=top_precision) - jnp.einsum(formula, gate_imag, imag_part, precision=top_precision)
    out_imag = jnp.einsum(formula, gate_real, imag_part, precision=top_precision) + jnp.einsum(formula, gate_imag, real_part, precision=top_precision)
    return out_real, out_imag


def apply_gate(real_part, imag_part, gate_real, gate_imag, offset_bits):
    amount = real_part.shape[0]
    if offset_bits == 0:
        shaped = (amount // 128, 128)
        formula = "ij,aj->ai"
    else:
        shaped = (amount // (128 << offset_bits), 128, 1 << offset_bits)
        formula = "ij,ajb->aib"
    out_real, out_imag = twisted(formula, gate_real, gate_imag, real_part.reshape(shaped), imag_part.reshape(shaped))
    return out_real.reshape(amount), out_imag.reshape(amount)


def controlled(real_part, imag_part, ctrl_gate, control_bits):
    empty_block = jnp.zeros_like(ctrl_gate[0])
    wide_real = jnp.block([[ctrl_gate[0], empty_block], [empty_block, ctrl_gate[0]]])
    wide_imag = jnp.block([[ctrl_gate[1], empty_block], [empty_block, ctrl_gate[1]]])
    new_real, new_imag = apply_gate(real_part, imag_part, wide_real, wide_imag, 0)
    amount = real_part.shape[0]
    chosen = jnp.repeat(control_bits.reshape(amount // 128, 2), 64, axis=1).reshape(amount) == 1
    return jnp.where(chosen, new_real, real_part), jnp.where(chosen, new_imag, imag_part)


def mid_matrix(mid_angles):
    cosine = jnp.cos(mid_angles[0])
    sine = jnp.sin(mid_angles[0])
    coef_real = jnp.stack([jnp.stack([cosine * jnp.cos(mid_angles[1]), -sine * jnp.cos(mid_angles[2])]), jnp.stack([sine * jnp.cos(mid_angles[2]), cosine * jnp.cos(mid_angles[1])])])
    coef_imag = jnp.stack([jnp.stack([cosine * jnp.sin(mid_angles[1]), -sine * jnp.sin(mid_angles[2])]), jnp.stack([-sine * jnp.sin(mid_angles[2]), -cosine * jnp.sin(mid_angles[1])])])
    return coef_real, coef_imag


def reference(amplitudes, layer_gates, ctrl_gate, control_mask, mid_angles):
    bits_local = LOCAL.bit_length() - 1
    slabs = jnp.transpose(amplitudes.reshape(2, N_HIGH * N_MID, LOCAL), (1, 0, 2))

    def early(slab):
        real_part, imag_part = apply_gate(slab[0], slab[1], layer_gates[0, 0], layer_gates[0, 1], 0)
        real_part, imag_part = apply_gate(real_part, imag_part, layer_gates[1, 0], layer_gates[1, 1], 7)
        return jnp.stack([real_part, imag_part])

    slabs = lax.map(early, slabs)
    moved = jnp.transpose(slabs, (1, 0, 2)).reshape(2, N_HIGH, N_MID, N_HIGH, LOCAL // N_HIGH)
    moved = jnp.transpose(moved, (0, 3, 2, 1, 4)).reshape(2, N_HIGH * N_MID, LOCAL)
    slabs = jnp.transpose(moved, (1, 0, 2))
    masks = control_mask.reshape(N_HIGH * N_MID, LOCAL // 64)

    def later(inputs):
        slab, control_bits = inputs
        real_part, imag_part = apply_gate(slab[0], slab[1], layer_gates[2, 0], layer_gates[2, 1], bits_local - 7)
        real_part, imag_part = controlled(real_part, imag_part, ctrl_gate, control_bits)
        real_part, imag_part = apply_gate(real_part, imag_part, layer_gates[3, 0], layer_gates[3, 1], 7)
        return jnp.stack([real_part, imag_part])

    slabs = lax.map(later, (slabs, masks))
    grid = jnp.transpose(slabs, (1, 0, 2)).reshape(2, N_HIGH, 2, N_MID // 2, LOCAL)
    coef_real, coef_imag = mid_matrix(mid_angles)
    real_part = grid[0]
    imag_part = grid[1]
    rows_real = []
    rows_imag = []
    for target in range(2):
        rows_real.append(coef_real[target, 0] * real_part[:, 0] - coef_imag[target, 0] * imag_part[:, 0] + coef_real[target, 1] * real_part[:, 1] - coef_imag[target, 1] * imag_part[:, 1])
        rows_imag.append(coef_real[target, 0] * imag_part[:, 0] + coef_imag[target, 0] * real_part[:, 0] + coef_real[target, 1] * imag_part[:, 1] + coef_imag[target, 1] * real_part[:, 1])
    out_real = jnp.stack(rows_real, 1)
    out_imag = jnp.stack(rows_imag, 1)
    return jnp.stack([out_real, out_imag]).reshape(2, N_HIGH, N_MID, LOCAL)
```

```python
import functools

import jax
import jax.numpy as jnp
from jax import lax
from jax.experimental import pallas as pl
from jax.experimental.pallas import tpu as pltpu
from jax.sharding import PartitionSpec as P

LANES = 128
HALF = 64
VMEM_LIMIT = 48 * 1024 * 1024
COST = pl.CostEstimate(flops=1, bytes_accessed=1, transcendentals=0)


def split_two(value):
    high = value.astype(jnp.bfloat16)
    low = (value - high.astype(jnp.float32)).astype(jnp.bfloat16)
    return high, low


def matmul(left, right):
    return lax.dot_general(left, right, (((1,), (0,)), ((), ())), preferred_element_type=jnp.float32)


def matmul_nt(left, right):
    return lax.dot_general(left, right, (((1,), (1,)), ((), ())), preferred_element_type=jnp.float32)


def right_gate(value, gate_high, gate_low):
    high, low = split_two(value)
    return matmul_nt(high, gate_high) + (matmul_nt(low, gate_high) + matmul_nt(high, gate_low))


def times_i(value):
    lane = lax.broadcasted_iota(jnp.int32, value.shape, 1)
    turned = pltpu.roll(value, HALF, 1)
    return jnp.where(lane < HALF, -turned, turned)


def left_operand(gate_ref):
    real_high, real_low = split_two(gate_ref[0, 0])
    imag_high, imag_low = split_two(gate_ref[0, 1])
    empty = jnp.zeros_like(real_low)
    return jnp.concatenate(
        [
            jnp.concatenate([real_high, real_high], axis=1),
            jnp.concatenate([imag_high, imag_high], axis=1),
            jnp.concatenate([real_low, empty], axis=1),
            jnp.concatenate([imag_low, empty], axis=1),
        ],
        axis=0,
    )


def left_gate(gate, value):
    product = matmul(gate, jnp.concatenate(split_two(value), axis=0))
    real = product[:LANES] + product[2 * LANES : 3 * LANES]
    imag = product[LANES : 2 * LANES] + product[3 * LANES :]
    return [
        real[:, begin : begin + LANES] + times_i(imag[:, begin : begin + LANES]) for begin in (0, LANES)
    ]


def early_kernel(blocks, tail, who_ref, x_ref, gate_a_ref, gate_b_ref, mask_ref, *refs):
    part_ref, zero_ref, one_ref, wide_high, wide_low, left = refs[-6:]
    step = pl.program_id(0)
    rows = blocks * LANES

    @pl.when(step == 0)
    def _():
        real, imag = gate_a_ref[0, 0], gate_a_ref[0, 1]
        pieces = []
        for begin in (0, HALF):
            piece_real, piece_imag = real[begin : begin + HALF], imag[begin : begin + HALF]
            pieces.append(jnp.concatenate([piece_real, -piece_imag], axis=1))
            pieces.append(jnp.concatenate([piece_imag, piece_real], axis=1))
        wide_high[...], wide_low[...] = split_two(jnp.concatenate(pieces, axis=0))
        left[...] = left_operand(gate_b_ref)
        if tail:
            mask = mask_ref[...].astype(jnp.float32)
            begin = part_ref.shape[0] - tail
            part_ref[pl.ds(begin, tail // 2)] = mask[:, :LANES]
            part_ref[pl.ds(begin + tail // 2, tail // 2)] = mask[:, LANES:]

    value = jnp.concatenate([x_ref[part, 0].reshape(rows, LANES) for part in range(2)], axis=1)
    value = right_gate(value, wide_high[...], wide_low[...])
    for block in range(blocks):
        zero, one = left_gate(left[...], value[block * LANES : (block + 1) * LANES])
        part_ref[pl.ds(pl.multiple_of(step * rows, rows) + block * LANES, LANES)] = zero
        zero_ref[0, pl.ds(block * LANES, LANES)] = zero
        one_ref[0, pl.ds(block * LANES, LANES)] = one


def early(who, x, gates, mask, apart, carried):
    groups, blocks = x.shape[1], x.shape[2]
    rows = blocks * LANES
    steps = 2 if blocks % 2 == 0 else 1
    tail = 2 * mask.shape[0] if apart == 0 else 0
    full = jax.ShapeDtypeStruct((groups, rows, LANES), jnp.float32)
    full_spec = pl.BlockSpec((1, rows // steps, LANES), lambda g, who: (who[0] ^ apart, g, 0))
    return pl.pallas_call(
        functools.partial(early_kernel, blocks // steps, tail),
        grid_spec=pltpu.PrefetchScalarGridSpec(
            num_scalar_prefetch=1,
            grid=(steps,),
            in_specs=[
                pl.BlockSpec((2, 1, blocks // steps, LANES, LANES), lambda g, who: (0, who[0] ^ apart, g, 0, 0)),
                pl.BlockSpec((1, 2, LANES, LANES), lambda g, who: (0, 0, 0, 0)),
                pl.BlockSpec((1, 2, LANES, LANES), lambda g, who: (1, 0, 0, 0)),
                pl.BlockSpec(mask.shape, lambda g, who: (0, 0)),
            ]
            + [pl.BlockSpec(memory_space=pl.ANY)] * len(carried),
            out_specs=[pl.BlockSpec((rows + tail, LANES), lambda g, who: (0, 0)), full_spec, full_spec],
            scratch_shapes=[
                pltpu.VMEM((2 * LANES, 2 * LANES), jnp.bfloat16),
                pltpu.VMEM((2 * LANES, 2 * LANES), jnp.bfloat16),
                pltpu.VMEM((4 * LANES, 2 * LANES), jnp.bfloat16),
            ],
        ),
        out_shape=[jax.ShapeDtypeStruct((rows + tail, LANES), jnp.float32), full, full],
        input_output_aliases={5: 1, 6: 2} if carried else {},
        compiler_params=pltpu.CompilerParams(vmem_limit_bytes=VMEM_LIMIT),
        cost_estimate=COST,
        name="early",
    )(who, x, gates, gates, mask, *carried)


def mix(coef_ref, at, value):
    return coef_ref[at] * value + coef_ref[at + 1] * times_i(value)


def late_kernel(half, parts, outs, *refs):
    sources = refs[:parts]
    gate_a_ref, gate_b_ref, ctrl_ref = refs[parts : parts + 3]
    held, control, left_a, left_b, right = refs[-5:]
    targets = refs[-5 - outs : -5]
    extra = refs[parts + 3 : -5 - outs]
    total = held.shape[0]
    stride = total // LANES

    left_a[...] = left_operand(gate_a_ref)
    left_b[...] = left_operand(gate_b_ref)
    high, low = split_two(ctrl_ref[...])
    right[...] = jnp.concatenate(
        [jnp.concatenate([high, high], axis=1), jnp.concatenate([low, jnp.zeros_like(low)], axis=1)], axis=0
    )
    if parts == 1:
        control[...] = extra[0][...].astype(jnp.float32)
        held[...] = sources[0][...]
    else:
        who_ref, own_ref, coef_ref = extra
        rows = total // parts
        tail = control.shape[0]
        control[:, :LANES] = sources[0][pl.ds(rows, tail), :]
        control[:, LANES:] = sources[0][pl.ds(rows + tail, tail), :]
        for apart in range(parts):
            held[pl.ds(pl.multiple_of((who_ref[0] ^ apart) * rows, rows), rows), :] = sources[apart][pl.ds(0, rows), :]

    @pl.loop(0, stride // 4)
    def _(step):
        for pair in range(2):
            first = step * 4 + pair * 2
            places = [pl.ds(first + side, LANES, stride=stride) for side in range(2)]
            value = jnp.concatenate([held[place, :] for place in places], axis=1)
            for place, piece in zip(places, left_gate(left_a[...], value)):
                held[place, :] = piece

    blocks = 4
    here = lax.broadcasted_iota(jnp.int32, (LANES, 2 * LANES), 0)
    there = lax.broadcasted_iota(jnp.int32, (LANES, 2 * LANES), 1)
    picked = there == 2 * here + half
    ones = jnp.ones((2 * LANES, LANES), jnp.bfloat16)
    span = total // outs

    for out in range(outs):
        target = targets[out]

        @pl.loop(0, span // (blocks * LANES))
        def _(step):
            begin = pl.multiple_of(step * (blocks * LANES), blocks * LANES)
            value = held[pl.ds(out * span + begin, blocks * LANES), :]
            acted = matmul_nt(jnp.concatenate(split_two(value), axis=1), right[...])
            acted = acted[:, :LANES] + acted[:, LANES:]
            chosen = []
            for block in range(blocks):
                row = control[pl.ds(out * (span // LANES) + step * blocks + block, 1), :]
                chosen.append(jnp.where(picked, jnp.broadcast_to(row, picked.shape), 0.0))
            chosen = matmul(jnp.concatenate(chosen, axis=0).astype(jnp.bfloat16), ones)
            value = jnp.where(chosen > 0.5, acted, value)
            for block in range(0, blocks, 2):
                both = jnp.concatenate(
                    [value[(block + side) * LANES : (block + side + 1) * LANES] for side in range(2)], axis=1
                )
                for side, piece in enumerate(left_gate(left_b[...], both)):
                    place = pl.ds(begin + (block + side) * LANES, LANES)
                    if parts > 1:
                        piece = mix(coef_ref, 0, own_ref[place, :]) + mix(coef_ref, 2, piece)
                    target[place, :] = piece


def late(sources, gates, ctrl, half, outs, *extra):
    parts = len(sources)
    total = sources[-1].shape[0] * parts
    vmem = pl.BlockSpec(memory_space=pltpu.VMEM)
    smem = pl.BlockSpec(memory_space=pltpu.SMEM)
    gate_specs = [pl.BlockSpec((1, 2, LANES, LANES), lambda g, at=at: (at, 0, 0, 0)) for at in (2, 3)]
    return pl.pallas_call(
        functools.partial(late_kernel, half, parts, outs),
        grid=(1,),
        in_specs=[vmem] * parts + gate_specs + [vmem] + ([vmem] if parts == 1 else [smem, vmem, smem]),
        out_specs=[vmem] * outs,
        out_shape=[jax.ShapeDtypeStruct((total // outs, LANES), jnp.float32)] * outs,
        scratch_shapes=[
            pltpu.VMEM((total, LANES), jnp.float32),
            pltpu.VMEM((total // LANES, 2 * LANES), jnp.float32),
            pltpu.VMEM((4 * LANES, 2 * LANES), jnp.bfloat16),
            pltpu.VMEM((4 * LANES, 2 * LANES), jnp.bfloat16),
            pltpu.VMEM((2 * LANES, 2 * LANES), jnp.bfloat16),
        ],
        compiler_params=pltpu.CompilerParams(vmem_limit_bytes=VMEM_LIMIT),
        cost_estimate=COST,
        name="late",
    )(*sources, gates, gates, ctrl, *extra)


def final_kernel(zero_ref, own_ref, other_ref, coef_ref, *refs):
    out_ref = refs[-1]
    zero = zero_ref[...]
    one = mix(coef_ref, 0, own_ref[...]) + mix(coef_ref, 2, other_ref[...])
    lane = lax.broadcasted_iota(jnp.int32, zero.shape, 1)
    out_ref[0] = jnp.where(lane < HALF, zero, pltpu.roll(one, HALF, 1))
    out_ref[1] = jnp.where(lane < HALF, pltpu.roll(zero, HALF, 1), one)


def final(zero, own, other, coefs, part, carried):
    total, rows = zero.shape[0], own.shape[0]
    steps = 2
    size = rows // steps
    here = pl.BlockSpec((size, LANES), lambda g: (g, 0))
    return pl.pallas_call(
        final_kernel,
        grid=(steps,),
        in_specs=[
            pl.BlockSpec((size, LANES), lambda g: (part * steps + g, 0)),
            here,
            here,
            pl.BlockSpec(memory_space=pltpu.SMEM),
        ]
        + [pl.BlockSpec(memory_space=pl.ANY)] * len(carried),
        out_specs=pl.BlockSpec((2, size, LANES), lambda g: (0, part * steps + g, 0)),
        out_shape=jax.ShapeDtypeStruct((2, total, LANES), jnp.float32),
        input_output_aliases={4: 0} if carried else {},
        compiler_params=pltpu.CompilerParams(vmem_limit_bytes=VMEM_LIMIT),
        cost_estimate=COST,
        name="final",
    )(zero, own, other, coefs, *carried)


def coefficients(mid_angles, parity):
    cosine, sine = jnp.cos(mid_angles), jnp.sin(mid_angles)
    sign = (1 - 2 * parity).astype(jnp.float32)
    return jnp.stack(
        [cosine[0] * cosine[1], sign * (cosine[0] * sine[1]), -sign * (sine[0] * cosine[2]), -sine[0] * sine[2]]
    )


def wide_ctrl(ctrl_gate):
    return jnp.block([[ctrl_gate[0], -ctrl_gate[1]], [ctrl_gate[1], ctrl_gate[0]]])


def body(amplitudes, layer_gates, ctrl_gate, control_mask, mid_angles):
    amount = amplitudes.shape[-1]
    total = amount // LANES
    groups = lax.axis_size("high")
    mid = lax.axis_size("mid")
    top_bit = mid.bit_length() - 2
    parity = lax.axis_index("mid") >> top_bit & 1
    who = lax.axis_index("high").astype(jnp.int32).reshape(1)

    def partner(value, apart=0):
        pairs = [
            (high * mid + at, (high ^ apart) * mid + (at ^ 1 << top_bit)) for high in range(groups) for at in range(mid)
        ]
        return lax.ppermute(value, ("high", "mid"), pairs)

    def trade(value):
        return lax.all_to_all(value, "high", split_axis=0, concat_axis=0, tiled=True).reshape(total, LANES)

    x = amplitudes.reshape(2, groups, total // groups // LANES, LANES, LANES)
    mask = control_mask.reshape(total // LANES, 2 * LANES)
    carried, away = (), []
    for apart in range(groups):
        part, *carried = early(who, x, layer_gates, mask, apart, carried)
        away.append(partner(part, apart))
    zero, one = carried
    ctrl = wide_ctrl(ctrl_gate)
    coefs = coefficients(mid_angles, parity)
    outs = 4
    one = trade(one)
    own_one = late([one], layer_gates, ctrl, 1, outs, mask)
    other_one = [partner(piece) for piece in own_one]
    zero, _ = lax.optimization_barrier((zero, one))
    (own_zero,) = late([trade(zero)], layer_gates, ctrl, 0, 1, mask)
    (mixed,) = late(away, layer_gates, ctrl, 0, 1, who, own_zero, coefs)
    result = ()
    for at in range(outs):
        result = (final(mixed, own_one[at], other_one[at], coefs, at, result),)
    return result[0].reshape(2, 1, 1, amount)


def solution(mesh):
    placed = (P(None, "high", "mid", None), P(), P(), P("high", "mid", None), P())
    return jax.shard_map(
        body, mesh=mesh, in_specs=placed, out_specs=P(None, "high", "mid", None), check_vma=False
    )
```

```python
import functools

import jax
import jax.numpy as jnp
from jax import lax
from jax.experimental import pallas as pl
from jax.experimental.pallas import tpu as pltpu
from jax.sharding import PartitionSpec as P

LANES = 128
HALF = 64
VMEM_LIMIT = 60 * 1024 * 1024
COST = pl.CostEstimate(flops=1, bytes_accessed=1, transcendentals=0)


def split_two(value):
    high = value.astype(jnp.bfloat16)
    low = (value - high.astype(jnp.float32)).astype(jnp.bfloat16)
    return high, low


def matmul(left, right):
    return lax.dot_general(left, right, (((1,), (0,)), ((), ())), preferred_element_type=jnp.float32)


def matmul_nt(left, right):
    return lax.dot_general(left, right, (((1,), (1,)), ((), ())), preferred_element_type=jnp.float32)


def right_gate(value, gate_high, gate_low):
    high, low = split_two(value)
    return matmul_nt(high, gate_high) + (matmul_nt(low, gate_high) + matmul_nt(high, gate_low))


def times_i(value):
    lane = lax.broadcasted_iota(jnp.int32, value.shape, 1)
    turned = pltpu.roll(value, HALF, 1)
    return jnp.where(lane < HALF, -turned, turned)


def left_operand(gate_ref):
    real_high, real_low = split_two(gate_ref[0, 0])
    imag_high, imag_low = split_two(gate_ref[0, 1])
    empty = jnp.zeros_like(real_low)
    return jnp.concatenate(
        [
            jnp.concatenate([real_high, real_high], axis=1),
            jnp.concatenate([imag_high, imag_high], axis=1),
            jnp.concatenate([real_low, empty], axis=1),
            jnp.concatenate([imag_low, empty], axis=1),
        ],
        axis=0,
    )


def left_gate(gate, value):
    product = matmul(gate, jnp.concatenate(split_two(value), axis=0))
    real = product[:LANES] + product[2 * LANES : 3 * LANES]
    imag = product[LANES : 2 * LANES] + product[3 * LANES :]
    return [
        real[:, begin : begin + LANES] + times_i(imag[:, begin : begin + LANES]) for begin in (0, LANES)
    ]


def early_kernel(blocks, tail, who_ref, x_ref, gate_a_ref, gate_b_ref, mask_ref, *refs):
    part_ref, pair_ref, wide_high, wide_low, left = refs[-5:]
    step = pl.program_id(0)
    rows = blocks * LANES

    @pl.when(step == 0)
    def _():
        real, imag = gate_a_ref[0, 0], gate_a_ref[0, 1]
        pieces = []
        for begin in (0, HALF):
            piece_real, piece_imag = real[begin : begin + HALF], imag[begin : begin + HALF]
            pieces.append(jnp.concatenate([piece_real, -piece_imag], axis=1))
            pieces.append(jnp.concatenate([piece_imag, piece_real], axis=1))
        wide_high[...], wide_low[...] = split_two(jnp.concatenate(pieces, axis=0))
        left[...] = left_operand(gate_b_ref)
        if tail:
            part_ref[pl.ds(part_ref.shape[0] - tail, tail)] = mask_ref[...].astype(jnp.float32)

    value = jnp.concatenate([x_ref[part, 0].reshape(rows, LANES) for part in range(2)], axis=1)
    value = right_gate(value, wide_high[...], wide_low[...])
    for block in range(blocks):
        zero, one = left_gate(left[...], value[block * LANES : (block + 1) * LANES])
        part_ref[pl.ds(pl.multiple_of(step * rows, rows) + block * LANES, LANES)] = zero
        pair_ref[0, pl.ds(block * LANES, LANES)] = zero
        pair_ref[1, pl.ds(block * LANES, LANES)] = one


def early(who, x, gates, mask, apart):
    groups, blocks = x.shape[1], x.shape[2]
    rows = blocks * LANES
    steps = 2 if blocks % 2 == 0 else 1
    tail = mask.shape[0] if apart == 0 else 0
    return pl.pallas_call(
        functools.partial(early_kernel, blocks // steps, tail),
        grid_spec=pltpu.PrefetchScalarGridSpec(
            num_scalar_prefetch=1,
            grid=(steps,),
            in_specs=[
                pl.BlockSpec((2, 1, blocks // steps, LANES, LANES), lambda g, who: (0, who[0] ^ apart, g, 0, 0)),
                pl.BlockSpec((1, 2, LANES, LANES), lambda g, who: (0, 0, 0, 0)),
                pl.BlockSpec((1, 2, LANES, LANES), lambda g, who: (1, 0, 0, 0)),
                pl.BlockSpec(mask.shape, lambda g, who: (0, 0)),
            ],
            out_specs=[
                pl.BlockSpec((rows + tail, LANES), lambda g, who: (0, 0)),
                pl.BlockSpec((2, rows // steps, LANES), lambda g, who: (0, g, 0)),
            ],
            scratch_shapes=[
                pltpu.VMEM((2 * LANES, 2 * LANES), jnp.bfloat16),
                pltpu.VMEM((2 * LANES, 2 * LANES), jnp.bfloat16),
                pltpu.VMEM((4 * LANES, 2 * LANES), jnp.bfloat16),
            ],
        ),
        out_shape=[
            jax.ShapeDtypeStruct((rows + tail, LANES), jnp.float32),
            jax.ShapeDtypeStruct((2, rows, LANES), jnp.float32),
        ],
        compiler_params=pltpu.CompilerParams(vmem_limit_bytes=VMEM_LIMIT),
        cost_estimate=COST,
        name="early",
    )(who, x, gates, gates, mask)


def mix(coef_ref, at, value):
    return coef_ref[at] * value + coef_ref[at + 1] * times_i(value)


def late_kernel(half, parts, outs, mixed, *refs):
    sources = refs[:parts]
    gate_a_ref, gate_b_ref, ctrl_ref, who_ref = refs[parts : parts + 4]
    held, control, left_a, left_b, right = refs[-5:]
    targets = refs[-5 - outs : -5]
    extra = refs[parts + 4 : -5 - outs]
    total = held.shape[0]
    stride = total // LANES
    rows = total // parts

    left_a[...] = left_operand(gate_a_ref)
    left_b[...] = left_operand(gate_b_ref)
    high, low = split_two(ctrl_ref[...])
    right[...] = jnp.concatenate(
        [jnp.concatenate([high, high], axis=1), jnp.concatenate([low, jnp.zeros_like(low)], axis=1)], axis=0
    )
    if mixed:
        own_ref, coef_ref = extra
        control[...] = sources[0][pl.ds(rows, control.shape[0]), :]
    else:
        control[...] = extra[0][...].astype(jnp.float32)
    for apart in range(parts):
        place = pl.multiple_of((who_ref[0] ^ apart) * rows, rows)
        held[pl.ds(place, rows), :] = sources[apart][pl.ds(0, rows), :] if mixed else sources[apart][0]

    @pl.loop(0, stride // 4)
    def _(step):
        for pair in range(2):
            first = step * 4 + pair * 2
            places = [pl.ds(first + side, LANES, stride=stride) for side in range(2)]
            value = jnp.concatenate([held[place, :] for place in places], axis=1)
            for place, piece in zip(places, left_gate(left_a[...], value)):
                held[place, :] = piece

    blocks = 4
    here = lax.broadcasted_iota(jnp.int32, (LANES, 2 * LANES), 0)
    there = lax.broadcasted_iota(jnp.int32, (LANES, 2 * LANES), 1)
    picked = there == 2 * here + half
    ones = jnp.ones((2 * LANES, LANES), jnp.bfloat16)
    span = total // outs

    for out in range(outs):
        target = targets[out]

        @pl.loop(0, span // (blocks * LANES))
        def _(step):
            begin = pl.multiple_of(step * (blocks * LANES), blocks * LANES)
            value = held[pl.ds(out * span + begin, blocks * LANES), :]
            acted = matmul_nt(jnp.concatenate(split_two(value), axis=1), right[...])
            acted = acted[:, :LANES] + acted[:, LANES:]
            chosen = []
            for block in range(blocks):
                at = (out * (span // LANES) + step * blocks + block) * 2
                row = jnp.concatenate([control[pl.ds(at, 1), :], control[pl.ds(at + 1, 1), :]], axis=1)
                chosen.append(jnp.where(picked, jnp.broadcast_to(row, picked.shape), 0.0))
            chosen = matmul(jnp.concatenate(chosen, axis=0).astype(jnp.bfloat16), ones)
            value = jnp.where(chosen > 0.5, acted, value)
            for block in range(0, blocks, 2):
                both = jnp.concatenate(
                    [value[(block + side) * LANES : (block + side + 1) * LANES] for side in range(2)], axis=1
                )
                for side, piece in enumerate(left_gate(left_b[...], both)):
                    place = pl.ds(begin + (block + side) * LANES, LANES)
                    if mixed:
                        piece = mix(coef_ref, 0, own_ref[place, :]) + mix(coef_ref, 2, piece)
                    target[place, :] = piece


def late(sources, gates, ctrl, who, half, outs, *extra):
    parts = len(sources)
    rows = sources[-1].shape[-2]
    total = rows * parts
    vmem = pl.BlockSpec(memory_space=pltpu.VMEM)
    smem = pl.BlockSpec(memory_space=pltpu.SMEM)
    source = vmem if len(extra) == 2 else pl.BlockSpec((1, rows, LANES), lambda g: (half, 0, 0))
    gate_specs = [pl.BlockSpec((1, 2, LANES, LANES), lambda g, at=at: (at, 0, 0, 0)) for at in (2, 3)]
    return pl.pallas_call(
        functools.partial(late_kernel, half, parts, outs, len(extra) == 2),
        grid=(1,),
        in_specs=[source] * parts + gate_specs + [vmem, smem] + ([vmem, smem] if len(extra) == 2 else [vmem]),
        out_specs=[vmem] * outs,
        out_shape=[jax.ShapeDtypeStruct((total // outs, LANES), jnp.float32)] * outs,
        scratch_shapes=[
            pltpu.VMEM((total, LANES), jnp.float32),
            pltpu.VMEM((total // HALF, LANES), jnp.float32),
            pltpu.VMEM((4 * LANES, 2 * LANES), jnp.bfloat16),
            pltpu.VMEM((4 * LANES, 2 * LANES), jnp.bfloat16),
            pltpu.VMEM((2 * LANES, 2 * LANES), jnp.bfloat16),
        ],
        compiler_params=pltpu.CompilerParams(vmem_limit_bytes=VMEM_LIMIT),
        cost_estimate=COST,
        name="late",
    )(*sources, gates, gates, ctrl, who, *extra)


def final_kernel(zero_ref, own_ref, other_ref, coef_ref, *refs):
    out_ref = refs[-1]
    zero = zero_ref[...]
    one = mix(coef_ref, 0, own_ref[...]) + mix(coef_ref, 2, other_ref[...])
    lane = lax.broadcasted_iota(jnp.int32, zero.shape, 1)
    out_ref[0] = jnp.where(lane < HALF, zero, pltpu.roll(one, HALF, 1))
    out_ref[1] = jnp.where(lane < HALF, pltpu.roll(zero, HALF, 1), one)


def final(zero, own, other, coefs, part, carried):
    total, rows = zero.shape[0], own.shape[0]
    steps = 2
    size = rows // steps
    here = pl.BlockSpec((size, LANES), lambda g: (g, 0))
    return pl.pallas_call(
        final_kernel,
        grid=(steps,),
        in_specs=[
            pl.BlockSpec((size, LANES), lambda g: (part * steps + g, 0)),
            here,
            here,
            pl.BlockSpec(memory_space=pltpu.SMEM),
        ]
        + [pl.BlockSpec(memory_space=pl.ANY)] * len(carried),
        out_specs=pl.BlockSpec((2, size, LANES), lambda g: (0, part * steps + g, 0)),
        out_shape=jax.ShapeDtypeStruct((2, total, LANES), jnp.float32),
        input_output_aliases={4: 0} if carried else {},
        compiler_params=pltpu.CompilerParams(vmem_limit_bytes=VMEM_LIMIT),
        cost_estimate=COST,
        name="final",
    )(zero, own, other, coefs, *carried)


def coefficients(mid_angles, parity):
    cosine, sine = jnp.cos(mid_angles), jnp.sin(mid_angles)
    sign = (1 - 2 * parity).astype(jnp.float32)
    return jnp.stack(
        [cosine[0] * cosine[1], sign * (cosine[0] * sine[1]), -sign * (sine[0] * cosine[2]), -sine[0] * sine[2]]
    )


def after(value, *others):
    return lax.optimization_barrier((value, *others))[0]


def wide_ctrl(ctrl_gate):
    return jnp.block([[ctrl_gate[0], -ctrl_gate[1]], [ctrl_gate[1], ctrl_gate[0]]])


def body(amplitudes, layer_gates, ctrl_gate, control_mask, mid_angles):
    amount = amplitudes.shape[-1]
    total = amount // LANES
    groups = lax.axis_size("high")
    mid = lax.axis_size("mid")
    top_bit = mid.bit_length() - 2
    parity = lax.axis_index("mid") >> top_bit & 1
    who = lax.axis_index("high").astype(jnp.int32).reshape(1)

    def move(value, apart, across=1):
        pairs = [
            (high * mid + at, (high ^ apart) * mid + (at ^ across << top_bit))
            for high in range(groups)
            for at in range(mid)
        ]
        return lax.ppermute(value, ("high", "mid"), pairs)

    x = amplitudes.reshape(2, groups, total // groups // LANES, LANES, LANES)
    mask = control_mask.reshape(total // HALF, LANES)
    away, pairs = [], []
    for apart in range(groups):
        part, pair = early(who, x, layer_gates, mask, apart)
        away.append(move(part, apart))
        pairs.append(pair)
    for apart in range(1, groups):
        pair = after(pairs[apart], away[0]) if apart == 1 else pairs[apart]
        pairs[apart] = move(pair, apart, 0)
    ctrl = wide_ctrl(ctrl_gate)
    coefs = coefficients(mid_angles, parity)
    outs = 4
    pairs[0] = after(pairs[0], *away[1:3])
    own_one = late(pairs, layer_gates, ctrl, who, 1, outs, mask)
    other_one = [move(piece, 0) for piece in own_one]
    (own_zero,) = late(pairs, layer_gates, ctrl, who, 0, 1, mask)
    (mixed,) = late(away, layer_gates, ctrl, who, 0, 1, own_zero, coefs)
    result = ()
    for at in range(outs):
        result = (final(mixed, own_one[at], other_one[at], coefs, at, result),)
    return result[0].reshape(2, 1, 1, amount)


def solution(mesh):
    placed = (P(None, "high", "mid", None), P(), P(), P("high", "mid", None), P())
    return jax.shard_map(
        body, mesh=mesh, in_specs=placed, out_specs=P(None, "high", "mid", None), check_vma=False
    )
```

```python
import functools

import jax
import jax.numpy as jnp
from jax import lax
from jax.experimental import pallas as pl
from jax.experimental.pallas import tpu as pltpu
from jax.sharding import PartitionSpec as P

LANES = 128
HALF = 64
EARLY_LIMIT = 60 * 1024 * 1024
LATE_LIMIT = 32 * 1024 * 1024
FINAL_LIMIT = 16 * 1024 * 1024
COST = pl.CostEstimate(flops=1, bytes_accessed=1, transcendentals=0)


def split_two(value):
    high = value.astype(jnp.bfloat16)
    low = (value - high.astype(jnp.float32)).astype(jnp.bfloat16)
    return high, low


def matmul(left, right):
    return lax.dot_general(left, right, (((1,), (0,)), ((), ())), preferred_element_type=jnp.float32)


def matmul_nt(left, right):
    return lax.dot_general(left, right, (((1,), (1,)), ((), ())), preferred_element_type=jnp.float32)


def right_gate(value, gate_high, gate_low):
    high, low = split_two(value)
    return matmul_nt(high, gate_high) + (matmul_nt(low, gate_high) + matmul_nt(high, gate_low))


def times_i(value):
    lane = lax.broadcasted_iota(jnp.int32, value.shape, 1)
    turned = pltpu.roll(value, HALF, 1)
    return jnp.where(lane < HALF, -turned, turned)


def left_operand(gate_ref):
    return jnp.concatenate(split_two(jnp.concatenate([gate_ref[0, 0], gate_ref[0, 1]], axis=1)), axis=0)


def left_gate(gate, value):
    turned = [times_i(value[:, begin : begin + LANES]) for begin in (0, LANES)]
    high, low = split_two(jnp.concatenate([value, jnp.concatenate(turned, axis=1)], axis=0))
    product = matmul(gate, high)
    product = product[:LANES] + (product[LANES:] + matmul(gate[:LANES], low))
    return product[:, :LANES], product[:, LANES:]


def early_kernel(tail, who_ref, x_ref, gate_a_ref, gate_b_ref, mask_ref, part_ref, pair_ref):
    rows = pair_ref.shape[1]
    if tail:
        part_ref[pl.ds(rows, tail)] = mask_ref[...].astype(jnp.float32)
    real, imag = gate_a_ref[0, 0], gate_a_ref[0, 1]
    pieces = []
    for begin in (0, HALF):
        piece_real, piece_imag = real[begin : begin + HALF], imag[begin : begin + HALF]
        pieces.append(jnp.concatenate([piece_real, -piece_imag], axis=1))
        pieces.append(jnp.concatenate([piece_imag, piece_real], axis=1))
    wide_high, wide_low = split_two(jnp.concatenate(pieces, axis=0))
    left = left_operand(gate_b_ref)
    value = jnp.concatenate([x_ref[part, 0].reshape(rows, LANES) for part in range(2)], axis=1)
    value = right_gate(value, wide_high, wide_low)
    for begin in range(0, rows, LANES):
        zero, one = left_gate(left, value[begin : begin + LANES])
        part_ref[pl.ds(begin, LANES)] = zero
        pair_ref[0, pl.ds(begin, LANES)] = zero
        pair_ref[1, pl.ds(begin, LANES)] = one


def early(who, x, gates, mask, apart, chunk, chunks):
    blocks = x.shape[2] // chunks
    rows = blocks * LANES
    tail = mask.shape[0] if apart == 0 and chunk == 0 else 0
    return pl.pallas_call(
        functools.partial(early_kernel, tail),
        grid_spec=pltpu.PrefetchScalarGridSpec(
            num_scalar_prefetch=1,
            grid=(1,),
            in_specs=[
                pl.BlockSpec((2, 1, blocks, LANES, LANES), lambda g, who: (0, who[0] ^ apart, chunk, 0, 0)),
                pl.BlockSpec((1, 2, LANES, LANES), lambda g, who: (0, 0, 0, 0)),
                pl.BlockSpec((1, 2, LANES, LANES), lambda g, who: (1, 0, 0, 0)),
                pl.BlockSpec(mask.shape, lambda g, who: (0, 0)),
            ],
            out_specs=[
                pl.BlockSpec((rows + tail, LANES), lambda g, who: (0, 0)),
                pl.BlockSpec((2, rows, LANES), lambda g, who: (0, 0, 0)),
            ],
        ),
        out_shape=[
            jax.ShapeDtypeStruct((rows + tail, LANES), jnp.float32),
            jax.ShapeDtypeStruct((2, rows, LANES), jnp.float32),
        ],
        compiler_params=pltpu.CompilerParams(vmem_limit_bytes=EARLY_LIMIT),
        cost_estimate=COST,
        name="early",
    )(who, x, gates, gates, mask)


def mix(coef_ref, at, value):
    return coef_ref[at] * value + coef_ref[at + 1] * times_i(value)


def late_kernel(half, places, sizes, mixed, *refs):
    sources = refs[: len(places)]
    gate_a_ref, gate_b_ref, ctrl_ref, who_ref = refs[len(places) : len(places) + 4]
    held, control, left_a, left_b, right = refs[-5:]
    targets = refs[-5 - len(sizes) : -5]
    extra = refs[len(places) + 4 : -5 - len(sizes)]
    total = held.shape[0]
    stride = total // LANES

    left_a[...] = left_operand(gate_a_ref)
    left_b[...] = left_operand(gate_b_ref)
    high, low = split_two(ctrl_ref[...])
    right[...] = jnp.concatenate(
        [jnp.concatenate([high, high], axis=1), jnp.concatenate([low, jnp.zeros_like(low)], axis=1)], axis=0
    )
    if mixed:
        own_ref, coef_ref = extra
        control[...] = sources[0][pl.ds(sources[0].shape[0] - control.shape[0], control.shape[0]), :]
    else:
        control[...] = extra[0][...].astype(jnp.float32)
    for source, (apart, span, begin, rows) in zip(sources, places):
        place = pl.ds(pl.multiple_of((who_ref[0] ^ apart) * span + begin, rows), rows)
        held[place, :] = source[pl.ds(0, rows), :] if mixed else source[0]

    @pl.loop(0, stride // 4)
    def _(step):
        for pair in range(2):
            first = step * 4 + pair * 2
            places = [pl.ds(first + side, LANES, stride=stride) for side in range(2)]
            value = jnp.concatenate([held[place, :] for place in places], axis=1)
            for place, piece in zip(places, left_gate(left_a[...], value)):
                held[place, :] = piece

    blocks = 4
    here = lax.broadcasted_iota(jnp.int32, (LANES, 2 * LANES), 0)
    there = lax.broadcasted_iota(jnp.int32, (LANES, 2 * LANES), 1)
    picked = there == 2 * here + half
    ones = jnp.ones((2 * LANES, LANES), jnp.bfloat16)
    for out, size in enumerate(sizes):
        target = targets[out]
        before = sum(sizes[:out])

        @pl.loop(0, size // (blocks * LANES))
        def _(step):
            begin = pl.multiple_of(step * (blocks * LANES), blocks * LANES)
            value = held[pl.ds(before + begin, blocks * LANES), :]
            acted = matmul_nt(jnp.concatenate(split_two(value), axis=1), right[...])
            acted = acted[:, :LANES] + acted[:, LANES:]
            chosen = []
            for block in range(blocks):
                at = (before // LANES + step * blocks + block) * 2
                row = jnp.concatenate([control[pl.ds(at, 1), :], control[pl.ds(at + 1, 1), :]], axis=1)
                chosen.append(jnp.where(picked, jnp.broadcast_to(row, picked.shape), 0.0))
            chosen = matmul(jnp.concatenate(chosen, axis=0).astype(jnp.bfloat16), ones)
            value = jnp.where(chosen > 0.5, acted, value)
            for block in range(0, blocks, 2):
                both = jnp.concatenate(
                    [value[(block + side) * LANES : (block + side + 1) * LANES] for side in range(2)], axis=1
                )
                for side, piece in enumerate(left_gate(left_b[...], both)):
                    place = pl.ds(begin + (block + side) * LANES, LANES)
                    if mixed:
                        piece = mix(coef_ref, 0, own_ref[place, :]) + mix(coef_ref, 2, piece)
                    target[place, :] = piece


def late(sources, places, gates, ctrl, who, half, sizes, *extra):
    mixed = len(extra) == 2
    total = sum(sizes)
    vmem = pl.BlockSpec(memory_space=pltpu.VMEM)
    smem = pl.BlockSpec(memory_space=pltpu.SMEM)
    source_specs = [
        vmem if mixed else pl.BlockSpec((1, *source.shape[1:]), lambda g: (half, 0, 0)) for source in sources
    ]
    gate_specs = [pl.BlockSpec((1, 2, LANES, LANES), lambda g, at=at: (at, 0, 0, 0)) for at in (2, 3)]
    return pl.pallas_call(
        functools.partial(late_kernel, half, places, sizes, mixed),
        grid=(1,),
        in_specs=source_specs + gate_specs + [vmem, smem] + ([vmem, smem] if mixed else [vmem]),
        out_specs=[vmem] * len(sizes),
        out_shape=[jax.ShapeDtypeStruct((size, LANES), jnp.float32) for size in sizes],
        scratch_shapes=[
            pltpu.VMEM((total, LANES), jnp.float32),
            pltpu.VMEM((total // HALF, LANES), jnp.float32),
            pltpu.VMEM((2 * LANES, 2 * LANES), jnp.bfloat16),
            pltpu.VMEM((2 * LANES, 2 * LANES), jnp.bfloat16),
            pltpu.VMEM((2 * LANES, 2 * LANES), jnp.bfloat16),
        ],
        compiler_params=pltpu.CompilerParams(vmem_limit_bytes=LATE_LIMIT),
        cost_estimate=COST,
        name="late",
    )(*sources, gates, gates, ctrl, who, *extra)


def final_kernel(zero_ref, own_ref, other_ref, coef_ref, *refs):
    out_ref = refs[-1]
    zero = zero_ref[...]
    one = mix(coef_ref, 0, own_ref[...]) + mix(coef_ref, 2, other_ref[...])
    lane = lax.broadcasted_iota(jnp.int32, zero.shape, 1)
    out_ref[0] = jnp.where(lane < HALF, zero, pltpu.roll(one, HALF, 1))
    out_ref[1] = jnp.where(lane < HALF, pltpu.roll(zero, HALF, 1), one)


def final(zero, own, other, coefs, before, carried):
    total, rows = zero.shape[0], own.shape[0]
    size = total // 8
    here = pl.BlockSpec((size, LANES), lambda g: (g, 0))
    return pl.pallas_call(
        final_kernel,
        grid=(rows // size,),
        in_specs=[
            pl.BlockSpec((size, LANES), lambda g: (before // size + g, 0)),
            here,
            here,
            pl.BlockSpec(memory_space=pltpu.SMEM),
        ]
        + [pl.BlockSpec(memory_space=pl.ANY)] * len(carried),
        out_specs=pl.BlockSpec((2, size, LANES), lambda g: (0, before // size + g, 0)),
        out_shape=jax.ShapeDtypeStruct((2, total, LANES), jnp.float32),
        input_output_aliases={4: 0} if carried else {},
        compiler_params=pltpu.CompilerParams(vmem_limit_bytes=FINAL_LIMIT),
        cost_estimate=COST,
        name="final",
    )(zero, own, other, coefs, *carried)


def coefficients(mid_angles, parity):
    cosine, sine = jnp.cos(mid_angles), jnp.sin(mid_angles)
    sign = (1 - 2 * parity).astype(jnp.float32)
    return jnp.stack(
        [cosine[0] * cosine[1], sign * (cosine[0] * sine[1]), -sign * (sine[0] * cosine[2]), -sine[0] * sine[2]]
    )


def after(value, *others):
    return lax.optimization_barrier((value, *others))[0]


def wide_ctrl(ctrl_gate):
    return jnp.block([[ctrl_gate[0], -ctrl_gate[1]], [ctrl_gate[1], ctrl_gate[0]]])


def body(amplitudes, layer_gates, ctrl_gate, control_mask, mid_angles):
    amount = amplitudes.shape[-1]
    total = amount // LANES
    groups = lax.axis_size("high")
    mid = lax.axis_size("mid")
    top_bit = mid.bit_length() - 2
    parity = lax.axis_index("mid") >> top_bit & 1
    who = lax.axis_index("high").astype(jnp.int32).reshape(1)

    def move(value, apart, across=1):
        pairs = [
            (high * mid + at, (high ^ apart) * mid + (at ^ across << top_bit))
            for high in range(groups)
            for at in range(mid)
        ]
        return lax.ppermute(value, ("high", "mid"), pairs)

    x = amplitudes.reshape(2, groups, total // groups // LANES, LANES, LANES)
    mask = control_mask.reshape(total // HALF, LANES)
    span = total // groups
    ctrl = wide_ctrl(ctrl_gate)
    coefs = coefficients(mid_angles, parity)
    places, away, pairs = [], [], []
    for apart in range(groups):
        chunks = 2 if apart < 2 and x.shape[2] % 2 == 0 else 1
        for chunk in range(chunks):
            part, pair = early(who, x, layer_gates, mask, apart, chunk, chunks)
            places.append((apart, span, chunk * (span // chunks), span // chunks))
            away.append(move(part, apart))
            pairs.append(pair)
    for at, (apart, *_) in enumerate(places):
        if apart == 1:
            pairs[at] = after(pairs[at], *[sent for sent, place in zip(away, places) if place[0] < 2])
        if apart:
            pairs[at] = move(pairs[at], apart, 0)
    sizes = [total // 8 * share for share in (2, 2, 2, 2)]
    own_one = late(pairs, places, layer_gates, ctrl, who, 1, sizes, mask)
    other_one = [move(piece, 0) for piece in own_one]
    (own_zero,) = late(pairs, places, layer_gates, ctrl, who, 0, [total], mask)
    (mixed,) = late(away, places, layer_gates, ctrl, who, 0, [total], own_zero, coefs)
    result = ()
    for at, size in enumerate(sizes):
        result = (final(mixed, own_one[at], other_one[at], coefs, sum(sizes[:at]), result),)
    return result[0].reshape(2, 1, 1, amount)


def solution(mesh):
    placed = (P(None, "high", "mid", None), P(), P(), P("high", "mid", None), P())
    return jax.shard_map(
        body, mesh=mesh, in_specs=placed, out_specs=P(None, "high", "mid", None), check_vma=False
    )
```

```python
import functools

import jax
import jax.numpy as jnp
from jax import lax
from jax.experimental import pallas as pl
from jax.experimental.pallas import tpu as pltpu
from jax.sharding import PartitionSpec as P

LANES = 128
HALF = 64
EARLY_LIMIT = 60 * 1024 * 1024
LATE_LIMIT = 32 * 1024 * 1024
FINAL_LIMIT = 16 * 1024 * 1024
COST = pl.CostEstimate(flops=1, bytes_accessed=1, transcendentals=0)


def split_two(value):
    high = value.astype(jnp.bfloat16)
    low = (value - high.astype(jnp.float32)).astype(jnp.bfloat16)
    return high, low


def matmul(left, right):
    return lax.dot_general(left, right, (((1,), (0,)), ((), ())), preferred_element_type=jnp.float32)


def matmul_nt(left, right):
    return lax.dot_general(left, right, (((1,), (1,)), ((), ())), preferred_element_type=jnp.float32)


def right_gate(value, gate_high, gate_low):
    high, low = split_two(value)
    return matmul_nt(high, gate_high) + (matmul_nt(low, gate_high) + matmul_nt(high, gate_low))


def times_i(value):
    lane = lax.broadcasted_iota(jnp.int32, value.shape, 1)
    turned = pltpu.roll(value, HALF, 1)
    return jnp.where(lane < HALF, -turned, turned)


def left_operand(gate_ref):
    return jnp.concatenate(split_two(jnp.concatenate([gate_ref[0, 0], gate_ref[0, 1]], axis=1)), axis=0)


def left_gate(gate, value):
    turned = [times_i(value[:, begin : begin + LANES]) for begin in (0, LANES)]
    high, low = split_two(jnp.concatenate([value, jnp.concatenate(turned, axis=1)], axis=0))
    product = matmul(gate, high)
    product = product[:LANES] + (product[LANES:] + matmul(gate[:LANES], low))
    return product[:, :LANES], product[:, LANES:]


def selectors():
    source = lax.broadcasted_iota(jnp.int32, (LANES, LANES), 0)
    lane = lax.broadcasted_iota(jnp.int32, (LANES, LANES), 1)
    return [(source == 2 * lane - shift).astype(jnp.bfloat16) for shift in (0, LANES)]


def early_kernel(tail, who_ref, x_ref, gate_a_ref, gate_b_ref, mask_ref, part_ref, *pair_refs):
    size = pair_refs[0].shape[1]
    rows = size * len(pair_refs)
    if tail:
        mask = mask_ref[...].astype(jnp.float32).astype(jnp.bfloat16)
        near, far = selectors()
        part_ref[pl.ds(rows, tail)] = matmul(mask[:tail], near) + matmul(mask[tail:], far)
    real, imag = gate_a_ref[0, 0], gate_a_ref[0, 1]
    pieces = []
    for begin in (0, HALF):
        piece_real, piece_imag = real[begin : begin + HALF], imag[begin : begin + HALF]
        pieces.append(jnp.concatenate([piece_real, -piece_imag], axis=1))
        pieces.append(jnp.concatenate([piece_imag, piece_real], axis=1))
    wide_high, wide_low = split_two(jnp.concatenate(pieces, axis=0))
    left = left_operand(gate_b_ref)
    value = jnp.concatenate([x_ref[part, 0].reshape(rows, LANES) for part in range(2)], axis=1)
    value = right_gate(value, wide_high, wide_low)
    for begin in range(0, rows, LANES):
        zero, one = left_gate(left, value[begin : begin + LANES])
        part_ref[pl.ds(begin, LANES)] = zero
        pair_refs[begin // size][0, pl.ds(begin % size, LANES)] = zero
        pair_refs[begin // size][1, pl.ds(begin % size, LANES)] = one


def early(who, x, gates, mask, apart, chunk, chunks, carrier, pieces):
    blocks = x.shape[2] // chunks
    rows = blocks * LANES
    tail = mask.shape[0] // 2 if carrier else 0
    return pl.pallas_call(
        functools.partial(early_kernel, tail),
        grid_spec=pltpu.PrefetchScalarGridSpec(
            num_scalar_prefetch=1,
            grid=(1,),
            in_specs=[
                pl.BlockSpec((2, 1, blocks, LANES, LANES), lambda g, who: (0, who[0] ^ apart, chunk, 0, 0)),
                pl.BlockSpec((1, 2, LANES, LANES), lambda g, who: (0, 0, 0, 0)),
                pl.BlockSpec((1, 2, LANES, LANES), lambda g, who: (1, 0, 0, 0)),
                pl.BlockSpec(mask.shape, lambda g, who: (0, 0)),
            ],
            out_specs=[
                pl.BlockSpec((rows + tail, LANES), lambda g, who: (0, 0)),
            ]
            + [pl.BlockSpec((2, rows // pieces, LANES), lambda g, who: (0, 0, 0))] * pieces,
        ),
        out_shape=[
            jax.ShapeDtypeStruct((rows + tail, LANES), jnp.float32),
        ]
        + [jax.ShapeDtypeStruct((2, rows // pieces, LANES), jnp.float32)] * pieces,
        compiler_params=pltpu.CompilerParams(vmem_limit_bytes=EARLY_LIMIT),
        cost_estimate=COST,
        name="early",
    )(who, x, gates, gates, mask)


def mix(coef_ref, at, value):
    return coef_ref[at] * value + coef_ref[at + 1] * times_i(value)


def late_kernel(half, places, sizes, mixed, *refs):
    sources = refs[: len(places)]
    gate_a_ref, gate_b_ref, ctrl_ref, who_ref = refs[len(places) : len(places) + 4]
    held, control, left_a, left_b, right = refs[-5:]
    targets = refs[-5 - len(sizes) : -5]
    extra = refs[len(places) + 4 : -5 - len(sizes)]
    total = held.shape[0]
    stride = total // LANES

    left_a[...] = left_operand(gate_a_ref)
    left_b[...] = left_operand(gate_b_ref)
    high, low = split_two(ctrl_ref[...])
    right[...] = jnp.concatenate(
        [jnp.concatenate([high, high], axis=1), jnp.concatenate([low, jnp.zeros_like(low)], axis=1)], axis=0
    )
    if mixed:
        own_ref, coef_ref = extra
        tail = control.shape[0] // 2
        (packed,) = [
            source[pl.ds(place[3], tail), :].astype(jnp.bfloat16)
            for source, place in zip(sources, places)
            if source.shape[0] > place[3]
        ]
        for at, selector in enumerate(selectors()):
            control[pl.ds(at * tail, tail)] = matmul_nt(packed, selector)
    else:
        control[...] = extra[0][...].astype(jnp.float32)
    for source, (apart, span, begin, rows) in zip(sources, places):
        place = pl.ds(pl.multiple_of((who_ref[0] ^ apart) * span + begin, rows), rows)
        held[place, :] = source[pl.ds(0, rows), :] if mixed else source[0]

    @pl.loop(0, stride // 4)
    def _(step):
        for pair in range(2):
            first = step * 4 + pair * 2
            places = [pl.ds(first + side, LANES, stride=stride) for side in range(2)]
            value = jnp.concatenate([held[place, :] for place in places], axis=1)
            for place, piece in zip(places, left_gate(left_a[...], value)):
                held[place, :] = piece

    blocks = 4
    here = lax.broadcasted_iota(jnp.int32, (LANES, 2 * LANES), 0)
    there = lax.broadcasted_iota(jnp.int32, (LANES, 2 * LANES), 1)
    picked = there == 2 * here + half
    ones = jnp.ones((2 * LANES, LANES), jnp.bfloat16)
    for out, size in enumerate(sizes):
        target = targets[out]
        before = sum(sizes[:out])

        @pl.loop(0, size // (blocks * LANES))
        def _(step):
            begin = pl.multiple_of(step * (blocks * LANES), blocks * LANES)
            value = held[pl.ds(before + begin, blocks * LANES), :]
            acted = matmul_nt(jnp.concatenate(split_two(value), axis=1), right[...])
            acted = acted[:, :LANES] + acted[:, LANES:]
            chosen = []
            for block in range(blocks):
                at = (before // LANES + step * blocks + block) * 2
                row = jnp.concatenate([control[pl.ds(at, 1), :], control[pl.ds(at + 1, 1), :]], axis=1)
                chosen.append(jnp.where(picked, jnp.broadcast_to(row, picked.shape), 0.0))
            chosen = matmul(jnp.concatenate(chosen, axis=0).astype(jnp.bfloat16), ones)
            value = jnp.where(chosen > 0.5, acted, value)
            for block in range(0, blocks, 2):
                both = jnp.concatenate(
                    [value[(block + side) * LANES : (block + side + 1) * LANES] for side in range(2)], axis=1
                )
                for side, piece in enumerate(left_gate(left_b[...], both)):
                    place = pl.ds(begin + (block + side) * LANES, LANES)
                    if mixed:
                        piece = mix(coef_ref, 0, own_ref[place, :]) + mix(coef_ref, 2, piece)
                    target[place, :] = piece


def late(sources, places, gates, ctrl, who, half, sizes, *extra):
    mixed = len(extra) == 2
    total = sum(sizes)
    vmem = pl.BlockSpec(memory_space=pltpu.VMEM)
    smem = pl.BlockSpec(memory_space=pltpu.SMEM)
    source_specs = [
        vmem if mixed else pl.BlockSpec((1, *source.shape[1:]), lambda g: (half, 0, 0)) for source in sources
    ]
    gate_specs = [pl.BlockSpec((1, 2, LANES, LANES), lambda g, at=at: (at, 0, 0, 0)) for at in (2, 3)]
    return pl.pallas_call(
        functools.partial(late_kernel, half, places, sizes, mixed),
        grid=(1,),
        in_specs=source_specs + gate_specs + [vmem, smem] + ([vmem, smem] if mixed else [vmem]),
        out_specs=[vmem] * len(sizes),
        out_shape=[jax.ShapeDtypeStruct((size, LANES), jnp.float32) for size in sizes],
        scratch_shapes=[
            pltpu.VMEM((total, LANES), jnp.float32),
            pltpu.VMEM((total // HALF, LANES), jnp.float32),
            pltpu.VMEM((2 * LANES, 2 * LANES), jnp.bfloat16),
            pltpu.VMEM((2 * LANES, 2 * LANES), jnp.bfloat16),
            pltpu.VMEM((2 * LANES, 2 * LANES), jnp.bfloat16),
        ],
        compiler_params=pltpu.CompilerParams(vmem_limit_bytes=LATE_LIMIT),
        cost_estimate=COST,
        name="late",
    )(*sources, gates, gates, ctrl, who, *extra)


def final_kernel(zero_ref, own_ref, other_ref, coef_ref, *refs):
    out_ref = refs[-1]
    zero = zero_ref[...]
    one = mix(coef_ref, 0, own_ref[...]) + mix(coef_ref, 2, other_ref[...])
    lane = lax.broadcasted_iota(jnp.int32, zero.shape, 1)
    out_ref[0] = jnp.where(lane < HALF, zero, pltpu.roll(one, HALF, 1))
    out_ref[1] = jnp.where(lane < HALF, pltpu.roll(zero, HALF, 1), one)


def final(zero, own, other, coefs, before, carried):
    total, rows = zero.shape[0], own.shape[0]
    size = total // 8
    here = pl.BlockSpec((size, LANES), lambda g: (g, 0))
    return pl.pallas_call(
        final_kernel,
        grid=(rows // size,),
        in_specs=[
            pl.BlockSpec((size, LANES), lambda g: (before // size + g, 0)),
            here,
            here,
            pl.BlockSpec(memory_space=pltpu.SMEM),
        ]
        + [pl.BlockSpec(memory_space=pl.ANY)] * len(carried),
        out_specs=pl.BlockSpec((2, size, LANES), lambda g: (0, before // size + g, 0)),
        out_shape=jax.ShapeDtypeStruct((2, total, LANES), jnp.float32),
        input_output_aliases={4: 0} if carried else {},
        compiler_params=pltpu.CompilerParams(vmem_limit_bytes=FINAL_LIMIT),
        cost_estimate=COST,
        name="final",
    )(zero, own, other, coefs, *carried)


def coefficients(mid_angles, parity):
    cosine, sine = jnp.cos(mid_angles), jnp.sin(mid_angles)
    sign = (1 - 2 * parity).astype(jnp.float32)
    return jnp.stack(
        [cosine[0] * cosine[1], sign * (cosine[0] * sine[1]), -sign * (sine[0] * cosine[2]), -sine[0] * sine[2]]
    )


def after(value, *others):
    return lax.optimization_barrier((value, *others))[0]


def wide_ctrl(ctrl_gate):
    return jnp.block([[ctrl_gate[0], -ctrl_gate[1]], [ctrl_gate[1], ctrl_gate[0]]])


def body(amplitudes, layer_gates, ctrl_gate, control_mask, mid_angles):
    amount = amplitudes.shape[-1]
    total = amount // LANES
    groups = lax.axis_size("high")
    mid = lax.axis_size("mid")
    top_bit = mid.bit_length() - 2
    parity = lax.axis_index("mid") >> top_bit & 1
    who = lax.axis_index("high").astype(jnp.int32).reshape(1)

    def move(value, apart, across=1):
        pairs = [
            (high * mid + at, (high ^ apart) * mid + (at ^ across << top_bit))
            for high in range(groups)
            for at in range(mid)
        ]
        return lax.ppermute(value, ("high", "mid"), pairs)

    x = amplitudes.reshape(2, groups, total // groups // LANES, LANES, LANES)
    mask = control_mask.reshape(total // HALF, LANES)
    span = total // groups
    ctrl = wide_ctrl(ctrl_gate)
    coefs = coefficients(mid_angles, parity)
    away, away_places, pairs, pair_places = [], [], [], []
    for apart in range(groups):
        chunks = 1
        pieces = 2 // chunks if apart == 1 and x.shape[2] % 2 == 0 else 1
        size = span // chunks
        for chunk in range(chunks):
            carrier = apart == 0
            part, *both = early(who, x, layer_gates, mask, apart, chunk, chunks, carrier, pieces)
            away.append(move(part, apart))
            away_places.append((apart, span, chunk * size, size))
            for piece, pair in enumerate(both):
                pairs.append(pair)
                pair_places.append((apart, span, chunk * size + piece * (size // pieces), size // pieces))
    first = [sent for sent, place in zip(away, away_places) if place[0] < 2]
    for at, (apart, *_) in enumerate(pair_places):
        if apart == 1:
            pairs[at] = after(pairs[at], *first)
        if apart:
            pairs[at] = move(pairs[at], apart, 0)
    sizes = [total // 8 * share for share in (2, 2, 2, 2)]
    own_one = late(pairs, pair_places, layer_gates, ctrl, who, 1, sizes, mask)
    other_one = [move(piece, 0) for piece in own_one]
    (own_zero,) = late(pairs, pair_places, layer_gates, ctrl, who, 0, [total], mask)
    (mixed,) = late(away, away_places, layer_gates, ctrl, who, 0, [total], own_zero, coefs)
    result = ()
    for at, size in enumerate(sizes):
        result = (final(mixed, own_one[at], other_one[at], coefs, sum(sizes[:at]), result),)
    return result[0].reshape(2, 1, 1, amount)


def solution(mesh):
    placed = (P(None, "high", "mid", None), P(), P(), P("high", "mid", None), P())
    return jax.shard_map(
        body, mesh=mesh, in_specs=placed, out_specs=P(None, "high", "mid", None), check_vma=False
    )
```

```python
import functools

import jax
import jax.numpy as jnp
from jax import lax
from jax.experimental import pallas as pl
from jax.experimental.pallas import tpu as pltpu
from jax.sharding import PartitionSpec as P

LANES = 128
HALF = 64
EARLY_LIMIT = 60 * 1024 * 1024
LATE_LIMIT = 32 * 1024 * 1024
FINAL_LIMIT = 16 * 1024 * 1024
COST = pl.CostEstimate(flops=1, bytes_accessed=1, transcendentals=0)


def split_two(value):
    high = value.astype(jnp.bfloat16)
    low = (value - high.astype(jnp.float32)).astype(jnp.bfloat16)
    return high, low


def matmul(left, right):
    return lax.dot_general(left, right, (((1,), (0,)), ((), ())), preferred_element_type=jnp.float32)


def matmul_nt(left, right):
    return lax.dot_general(left, right, (((1,), (1,)), ((), ())), preferred_element_type=jnp.float32)


def right_gate(value, gate_high, gate_low):
    high, low = split_two(value)
    return matmul_nt(high, gate_high) + (matmul_nt(low, gate_high) + matmul_nt(high, gate_low))


def times_i(value):
    lane = lax.broadcasted_iota(jnp.int32, value.shape, 1)
    turned = pltpu.roll(value, HALF, 1)
    return jnp.where(lane < HALF, -turned, turned)


def left_operand(gate_ref):
    return jnp.concatenate(split_two(jnp.concatenate([gate_ref[0, 0], gate_ref[0, 1]], axis=1)), axis=0)


def left_gate(gate, value):
    turned = [times_i(value[:, begin : begin + LANES]) for begin in (0, LANES)]
    high, low = split_two(jnp.concatenate([value, jnp.concatenate(turned, axis=1)], axis=0))
    product = matmul(gate, high)
    product = product[:LANES] + (product[LANES:] + matmul(gate[:LANES], low))
    return product[:, :LANES], product[:, LANES:]


def selectors():
    source = lax.broadcasted_iota(jnp.int32, (LANES, LANES), 0)
    lane = lax.broadcasted_iota(jnp.int32, (LANES, LANES), 1)
    return [(source == 2 * lane - shift).astype(jnp.bfloat16) for shift in (0, LANES)]


def wide_gate(gate_ref, halves):
    real, imag = gate_ref[0, 0], gate_ref[0, 1]
    pieces = []
    for begin in range(0, halves * HALF, HALF):
        piece_real, piece_imag = real[begin : begin + HALF], imag[begin : begin + HALF]
        pieces.append(jnp.concatenate([piece_real, -piece_imag], axis=1))
        pieces.append(jnp.concatenate([piece_imag, piece_real], axis=1))
    return split_two(jnp.concatenate(pieces, axis=0))


def first_kernel(who_ref, x_ref, gate_a_ref, gate_b_ref, mask_ref, part_ref):
    tail = mask_ref.shape[0] // 2
    rows = part_ref.shape[0] - tail
    mask = mask_ref[...].astype(jnp.float32).astype(jnp.bfloat16)
    near, far = selectors()
    part_ref[pl.ds(rows, tail)] = matmul(mask[:tail], near) + matmul(mask[tail:], far)
    left = left_operand(gate_b_ref)
    value = jnp.concatenate([x_ref[part, 0].reshape(rows, LANES) for part in range(2)], axis=1)
    value = right_gate(value, *wide_gate(gate_a_ref, 1))
    for begin in range(0, rows, 2 * LANES):
        both = [value[begin + side : begin + side + LANES] for side in (0, LANES)]
        for side, piece in zip((0, LANES), left_gate(left, jnp.concatenate(both, axis=1))):
            part_ref[pl.ds(begin + side, LANES)] = piece


def early_kernel(sent, who_ref, x_ref, gate_a_ref, gate_b_ref, *refs):
    pair_refs = refs[1:] if sent else refs
    size = pair_refs[0].shape[1]
    rows = size * len(pair_refs)
    left = left_operand(gate_b_ref)
    value = jnp.concatenate([x_ref[part, 0].reshape(rows, LANES) for part in range(2)], axis=1)
    value = right_gate(value, *wide_gate(gate_a_ref, 2))
    for begin in range(0, rows, LANES):
        zero, one = left_gate(left, value[begin : begin + LANES])
        if sent:
            refs[0][pl.ds(begin, LANES)] = zero
        pair_refs[begin // size][0, pl.ds(begin % size, LANES)] = zero
        pair_refs[begin // size][1, pl.ds(begin % size, LANES)] = one


def apart_kernel(who_ref, x_ref, gate_a_ref, gate_b_ref, zero_ref, one_ref):
    rows = zero_ref.shape[0]
    left = left_operand(gate_b_ref)
    value = jnp.concatenate([x_ref[part, 0].reshape(rows, LANES) for part in range(2)], axis=1)
    value = right_gate(value, *wide_gate(gate_a_ref, 2))
    for begin in range(0, rows, LANES):
        place = pl.ds(begin, LANES)
        zero_ref[place], one_ref[place] = left_gate(left, value[begin : begin + LANES])


def early_call(kernel, who, x, gates, apart, shapes, *extra):
    blocks = x.shape[2]

    def whole(shape):
        return pl.BlockSpec(shape, lambda g, who: (0,) * len(shape))

    return pl.pallas_call(
        kernel,
        grid_spec=pltpu.PrefetchScalarGridSpec(
            num_scalar_prefetch=1,
            grid=(1,),
            in_specs=[
                pl.BlockSpec((2, 1, blocks, LANES, LANES), lambda g, who: (0, who[0] ^ apart, 0, 0, 0)),
                pl.BlockSpec((1, 2, LANES, LANES), lambda g, who: (0, 0, 0, 0)),
                pl.BlockSpec((1, 2, LANES, LANES), lambda g, who: (1, 0, 0, 0)),
            ]
            + [whole(array.shape) for array in extra],
            out_specs=[whole(shape) for shape in shapes],
        ),
        out_shape=[jax.ShapeDtypeStruct(shape, jnp.float32) for shape in shapes],
        compiler_params=pltpu.CompilerParams(vmem_limit_bytes=EARLY_LIMIT),
        cost_estimate=COST,
        name="early",
    )(who, x, gates, gates, *extra)


def early(who, x, gates, mask, apart, pieces):
    rows = x.shape[2] * LANES
    pairs = [(2, rows // pieces, LANES)] * pieces
    if apart > 1:
        return early_call(apart_kernel, who, x, gates, apart, [(rows, LANES)] * 2)
    if apart:
        return early_call(functools.partial(early_kernel, True), who, x, gates, apart, [(rows, LANES)] + pairs)
    tail = mask.shape[0] // 2
    part = early_call(first_kernel, who, x, gates, apart, [(rows + tail, LANES)], mask)
    return part + early_call(functools.partial(early_kernel, False), who, x, gates, apart, pairs)


def mix(coef_ref, at, value):
    return coef_ref[at] * value + coef_ref[at + 1] * times_i(value)


def late_kernel(half, places, sizes, mixed, *refs):
    sources = refs[: len(places)]
    gate_a_ref, gate_b_ref, ctrl_ref, who_ref = refs[len(places) : len(places) + 4]
    held, control, left_a, left_b, right = refs[-5:]
    targets = refs[-5 - len(sizes) : -5]
    extra = refs[len(places) + 4 : -5 - len(sizes)]
    total = held.shape[0]
    stride = total // LANES

    left_a[...] = left_operand(gate_a_ref)
    left_b[...] = left_operand(gate_b_ref)
    high, low = split_two(ctrl_ref[...])
    right[...] = jnp.concatenate(
        [jnp.concatenate([high, high], axis=1), jnp.concatenate([low, jnp.zeros_like(low)], axis=1)], axis=0
    )
    if mixed:
        own_ref, coef_ref = extra
        tail = control.shape[0] // 2
        (packed,) = [
            source[pl.ds(place[3], tail), :].astype(jnp.bfloat16)
            for source, place in zip(sources, places)
            if source.shape[0] > place[3]
        ]
        for at, selector in enumerate(selectors()):
            control[pl.ds(at * tail, tail)] = matmul_nt(packed, selector)
    else:
        control[...] = extra[0][...].astype(jnp.float32)
    for source, (apart, span, begin, rows) in zip(sources, places):
        place = pl.ds(pl.multiple_of((who_ref[0] ^ apart) * span + begin, LANES), rows)
        held[place, :] = source[pl.ds(0, rows), :] if len(source.shape) == 2 else source[0]

    @pl.loop(0, stride // 4)
    def _(step):
        for pair in range(2):
            first = step * 4 + pair * 2
            places = [pl.ds(first + side, LANES, stride=stride) for side in range(2)]
            value = jnp.concatenate([held[place, :] for place in places], axis=1)
            for place, piece in zip(places, left_gate(left_a[...], value)):
                held[place, :] = piece

    blocks = 4
    here = lax.broadcasted_iota(jnp.int32, (LANES, 2 * LANES), 0)
    there = lax.broadcasted_iota(jnp.int32, (LANES, 2 * LANES), 1)
    picked = there == 2 * here + half
    ones = jnp.ones((2 * LANES, LANES), jnp.bfloat16)
    for out, size in enumerate(sizes):
        target = targets[out]
        before = sum(sizes[:out])

        @pl.loop(0, size // (blocks * LANES))
        def _(step):
            begin = pl.multiple_of(step * (blocks * LANES), blocks * LANES)
            value = held[pl.ds(before + begin, blocks * LANES), :]
            acted = matmul_nt(jnp.concatenate(split_two(value), axis=1), right[...])
            acted = acted[:, :LANES] + acted[:, LANES:]
            chosen = []
            for block in range(blocks):
                at = (before // LANES + step * blocks + block) * 2
                row = jnp.concatenate([control[pl.ds(at, 1), :], control[pl.ds(at + 1, 1), :]], axis=1)
                chosen.append(jnp.where(picked, jnp.broadcast_to(row, picked.shape), 0.0))
            chosen = matmul(jnp.concatenate(chosen, axis=0).astype(jnp.bfloat16), ones)
            value = jnp.where(chosen > 0.5, acted, value)
            for block in range(0, blocks, 2):
                both = jnp.concatenate(
                    [value[(block + side) * LANES : (block + side + 1) * LANES] for side in range(2)], axis=1
                )
                for side, piece in enumerate(left_gate(left_b[...], both)):
                    place = pl.ds(begin + (block + side) * LANES, LANES)
                    if mixed:
                        piece = mix(coef_ref, 0, own_ref[place, :]) + mix(coef_ref, 2, piece)
                    target[place, :] = piece


def late(sources, places, gates, ctrl, who, half, sizes, *extra):
    mixed = len(extra) == 2
    total = sum(sizes)
    vmem = pl.BlockSpec(memory_space=pltpu.VMEM)
    smem = pl.BlockSpec(memory_space=pltpu.SMEM)
    source_specs = [
        vmem if source.ndim == 2 else pl.BlockSpec((1, *source.shape[1:]), lambda g: (half, 0, 0)) for source in sources
    ]
    gate_specs = [pl.BlockSpec((1, 2, LANES, LANES), lambda g, at=at: (at, 0, 0, 0)) for at in (2, 3)]
    return pl.pallas_call(
        functools.partial(late_kernel, half, places, sizes, mixed),
        grid=(1,),
        in_specs=source_specs + gate_specs + [vmem, smem] + ([vmem, smem] if mixed else [vmem]),
        out_specs=[vmem] * len(sizes),
        out_shape=[jax.ShapeDtypeStruct((size, LANES), jnp.float32) for size in sizes],
        scratch_shapes=[
            pltpu.VMEM((total, LANES), jnp.float32),
            pltpu.VMEM((total // HALF, LANES), jnp.float32),
            pltpu.VMEM((2 * LANES, 2 * LANES), jnp.bfloat16),
            pltpu.VMEM((2 * LANES, 2 * LANES), jnp.bfloat16),
            pltpu.VMEM((2 * LANES, 2 * LANES), jnp.bfloat16),
        ],
        compiler_params=pltpu.CompilerParams(vmem_limit_bytes=LATE_LIMIT),
        cost_estimate=COST,
        name="late",
    )(*sources, gates, gates, ctrl, who, *extra)


def final_kernel(zero_ref, own_ref, other_ref, coef_ref, *refs):
    out_ref = refs[-1]
    zero = zero_ref[...]
    one = mix(coef_ref, 0, own_ref[...]) + mix(coef_ref, 2, other_ref[...])
    lane = lax.broadcasted_iota(jnp.int32, zero.shape, 1)
    out_ref[0] = jnp.where(lane < HALF, zero, pltpu.roll(one, HALF, 1))
    out_ref[1] = jnp.where(lane < HALF, pltpu.roll(zero, HALF, 1), one)


def final(zero, own, other, coefs, before, carried):
    total, rows = zero.shape[0], own.shape[0]
    size = total // 8
    here = pl.BlockSpec((size, LANES), lambda g: (g, 0))
    return pl.pallas_call(
        final_kernel,
        grid=(rows // size,),
        in_specs=[
            pl.BlockSpec((size, LANES), lambda g: (before // size + g, 0)),
            here,
            here,
            pl.BlockSpec(memory_space=pltpu.SMEM),
        ]
        + [pl.BlockSpec(memory_space=pl.ANY)] * len(carried),
        out_specs=pl.BlockSpec((2, size, LANES), lambda g: (0, before // size + g, 0)),
        out_shape=jax.ShapeDtypeStruct((2, total, LANES), jnp.float32),
        input_output_aliases={4: 0} if carried else {},
        compiler_params=pltpu.CompilerParams(vmem_limit_bytes=FINAL_LIMIT),
        cost_estimate=COST,
        name="final",
    )(zero, own, other, coefs, *carried)


def coefficients(mid_angles, parity):
    cosine, sine = jnp.cos(mid_angles), jnp.sin(mid_angles)
    sign = (1 - 2 * parity).astype(jnp.float32)
    return jnp.stack(
        [cosine[0] * cosine[1], sign * (cosine[0] * sine[1]), -sign * (sine[0] * cosine[2]), -sine[0] * sine[2]]
    )


def after(value, *others):
    return lax.optimization_barrier((value, *others))[0]


def wide_ctrl(ctrl_gate):
    return jnp.block([[ctrl_gate[0], -ctrl_gate[1]], [ctrl_gate[1], ctrl_gate[0]]])


def body(amplitudes, layer_gates, ctrl_gate, control_mask, mid_angles):
    amount = amplitudes.shape[-1]
    total = amount // LANES
    groups = lax.axis_size("high")
    mid = lax.axis_size("mid")
    top_bit = mid.bit_length() - 2
    parity = lax.axis_index("mid") >> top_bit & 1
    who = lax.axis_index("high").astype(jnp.int32).reshape(1)

    def move(value, apart, across=1):
        pairs = [
            (high * mid + at, (high ^ apart) * mid + (at ^ across << top_bit))
            for high in range(groups)
            for at in range(mid)
        ]
        return lax.ppermute(value, ("high", "mid"), pairs)

    x = amplitudes.reshape(2, groups, total // groups // LANES, LANES, LANES)
    mask = control_mask.reshape(total // HALF, LANES)
    span = total // groups
    ctrl = wide_ctrl(ctrl_gate)
    coefs = coefficients(mid_angles, parity)
    away, away_places, zeros, ones, places = [], [], [], [], []
    for apart in range(groups):
        pieces = 2 if apart == 1 and x.shape[2] % 2 == 0 else 1
        part, *both = early(who, x, layer_gates, mask, apart, pieces)
        away.append(move(part, apart))
        away_places.append((apart, span, 0, span))
        for piece, pair in enumerate(both):
            ones.append(pair)
            zeros.append(part if apart > 1 else pair)
            places.append((apart, span, piece * (span // pieces), span // pieces))
    for at, (apart, *_) in enumerate(places):
        if apart == 1:
            zeros[at] = ones[at] = move(after(ones[at], *away[:2]), apart, 0)
        elif apart:
            zeros[at] = move(after(zeros[at], *away[:2]), apart, 0)
            ones[at] = move(ones[at], apart, 0)
    sizes = [total // 8 * share for share in (2, 2, 2, 2)]
    own_one = late(ones, places, layer_gates, ctrl, who, 1, sizes, mask)
    other_one = [move(piece, 0) for piece in own_one]
    (own_zero,) = late(zeros, places, layer_gates, ctrl, who, 0, [total], mask)
    (mixed,) = late(away, away_places, layer_gates, ctrl, who, 0, [total], own_zero, coefs)
    result = ()
    for at, size in enumerate(sizes):
        result = (final(mixed, own_one[at], other_one[at], coefs, sum(sizes[:at]), result),)
    return result[0].reshape(2, 1, 1, amount)


def solution(mesh):
    placed = (P(None, "high", "mid", None), P(), P(), P("high", "mid", None), P())
    return jax.shard_map(
        body, mesh=mesh, in_specs=placed, out_specs=P(None, "high", "mid", None), check_vma=False
    )
```
